32 devices in a mesh: blocks: 2 (over x), depth: 4 (over y, core), angle: 4 (over z).
Axes of the slice: x: 2, y: 2, z: 4, core: 2. Of those that a mesh axis runs over, the one named last changes fastest.
Arguments:
- index_change: float32 [16, 256, 256], P(('blocks', 'depth')), parts along dimension 0, may hold values from -4 to 4
- measured: float32 [16, 256, 256], P(('blocks', 'angle')), parts along dimension 0, may hold values from 0.25 to 2
- angle_index: int32 [16, 2], P(('blocks', 'angle')), parts along dimension 0, may hold values from -25 to 25
- cutoff: int32 [1], replicated, may hold values from 32 to 128
Outputs:
- gradient: float32 [16, 256, 256], P(('blocks', 'depth'), 'angle'), parts along dimension 0
The draws below stay inside these ranges and needn't reach their ends.
There are 2 independent parts, one for each index of `blocks`. The reference program is written for one: setup_inputs(seed, part) draws one part's arguments, and reference() takes and returns one part's arrays. A program takes and returns all parts, laid end to end along the dimension named above; an argument that names none is the same for every part. Nothing has to cross between parts.
All inputs are finite; a program needn't handle non-finite values.
Results may differ from the reference program's by a relative error of at most 0.0003.
Values sent between devices are 32-bit elements; how exact they have to be, the bound alone decides.
A program may use at most 64 MiB of HBM per device.

```python
import math
import jax
import jax.numpy as jnp
from jax import lax

W = 256
NZ = 8
NANG = 8


def with_ends(drawn, own_key, least, largest):
    index_at = [jax.random.randint(jax.random.fold_in(own_key, axis), (), 0, length) for axis, length in enumerate(drawn.shape)]
    longest = drawn.shape.index(max(drawn.shape))
    next_to = index_at[:longest] + [(index_at[longest] + 1) % drawn.shape[longest]] + index_at[longest + 1:]
    return drawn.at[tuple(index_at)].set(least).at[tuple(next_to)].set(largest)


def block_scale(rng, dims, cuts, smallest, largest):
    level, own = 1.0, jax.random.fold_in(rng, 6)
    for position, blocks in cuts:
        steps = jnp.exp(jax.random.uniform(jax.random.fold_in(own, position), (blocks,), jnp.float32, smallest / len(cuts), largest / len(cuts)))
        level = level * jnp.repeat(steps, dims[position] // blocks).reshape([-1 if axis == position else 1 for axis in range(len(dims))])
    return level


def centred(rng, extent, scale, most, shards=(), held_as=jnp.bfloat16):
    entries = scale * jax.random.normal(rng, extent, jnp.float32)
    if shards:
        entries = entries * block_scale(rng, extent, shards, -0.22, 0.18)
    return jnp.clip(entries, -most, most).astype(held_as)


def setup_inputs(seed: int = 0, part: int = 0) -> dict:
    key_list = jax.random.split(jax.random.key(seed), 5)
    part_keys = jax.random.split(jax.random.fold_in(key_list[4], part), 5)
    return {
        "index_change": centred(part_keys[0], (NZ, W, W), 1.0, 4.0, ((0, 4),), jnp.float32),
        "measured": jnp.clip(0.25 + 1.75 * jax.random.uniform(part_keys[1], (NANG, W, W), jnp.float32) ** block_scale(part_keys[1], (NANG, W, W), ((0, 4),), -0.2, 0.2), 0.25, 2.0),
        "angle_index": with_ends(jax.random.randint(part_keys[2], (NANG, 2), 0 - W // 10, W // 10 + 1), jax.random.fold_in(part_keys[2], 1), 0 - W // 10, (W // 10 + 1) - 1).astype(jnp.int32),
        "cutoff": jax.random.randint(key_list[3], (1,), W // 8, W // 2 + 1).astype(jnp.int32),
    }


def reference(index_change, measured, angle_index, cutoff):
    index = jnp.arange(W, dtype=jnp.int32)
    freq = (index + W // 2) % W - W // 2
    frequency_sq = freq[:, None] * freq[:, None] + freq[None, :] * freq[None, :]
    phi = 13.0 / W * (jnp.sqrt(0.64 * W * W - frequency_sq.astype(jnp.float32)) - 0.8 * W)
    propagator = lax.complex(jnp.cos(phi), jnp.sin(phi))
    pupil = (frequency_sq <= cutoff[0] * cutoff[0]).astype(jnp.float32)
    screens = lax.complex(jnp.cos(0.25 * index_change), jnp.sin(0.25 * index_change))

    def one_angle(total, inputs):
        pair, target = inputs
        phase = 2.0 * math.pi / W * ((pair[0] * index[:, None] + pair[1] * index[None, :]) % W).astype(jnp.float32)
        incident = lax.complex(jnp.cos(phase), jnp.sin(phase))

        def forward_slice(field, screen):
            field = jnp.fft.ifft2(jnp.fft.fft2(field) * propagator) * screen
            return (field, field)
        bottom, fields = lax.scan(forward_slice, incident, screens)
        image = jnp.fft.ifft2(jnp.fft.fft2(bottom) * pupil)
        misfit = jnp.real(image) ** 2 + jnp.imag(image) ** 2 - target
        adjoint = jnp.fft.ifft2(jnp.fft.fft2(2.0 * misfit * image) * pupil)

        def backward_slice(adjoint, inputs):
            screen, field = inputs
            term = 0.25 * (jnp.real(field) * jnp.imag(adjoint) - jnp.imag(field) * jnp.real(adjoint))
            adjoint = jnp.fft.ifft2(jnp.fft.fft2(adjoint * jnp.conj(screen)) * jnp.conj(propagator))
            return (adjoint, term)
        unused, terms = lax.scan(backward_slice, adjoint, (screens, fields), reverse=True)
        return (total + terms, None)
    gradient, unused = lax.scan(one_angle, jnp.zeros((NZ, W, W), jnp.float32), (angle_index, measured))
    return gradient
```

```python
import functools
import math

import jax
import jax.numpy as jnp
import numpy as np
from jax import lax
from jax.experimental import pallas as pl
from jax.experimental.pallas import tpu as pltpu
from jax.sharding import PartitionSpec as P

screen_scale = 0.25
F32 = jnp.float32
BF16 = jnp.bfloat16


def tables(width):
    index = np.arange(width)
    turn = 2.0 * np.pi / width * (index[:, None] * index[None, :] % width)
    hartley = ((np.cos(turn) + np.sin(turn)) / math.sqrt(width)).astype(np.float32)
    high = hartley.astype(BF16)
    low = (hartley - high.astype(np.float32)).astype(BF16)
    freq = (index + width // 2) % width - width // 2
    square = (freq[:, None] ** 2 + freq[None, :] ** 2).astype(np.float64)
    phi = 13.0 / width * (np.sqrt(0.64 * width * width - square) - 0.8 * width)
    wave = np.stack([np.cos(phi), np.sin(phi)]).astype(np.float32)
    return (
        np.concatenate([high, high, low], 1),
        np.concatenate([high, high, low], 0),
        wave,
        square.astype(np.float32),
    )


def halves(value):
    high = value.astype(BF16)
    return high, (value - high.astype(F32)).astype(BF16)


def sincos_small(angle):
    sq = angle * angle
    cosine = 1.0 + sq * (
        -0.5 + sq * (1 / 24 + sq * (-1 / 720 + sq * (1 / 40320 - sq * (1 / 3628800))))
    )
    sine = angle * (
        1.0 + sq * (-1 / 6 + sq * (1 / 120 + sq * (-1 / 5040 + sq * (1 / 362880))))
    )
    return cosine, sine


def sincos_steps(steps, width):
    steps = steps & (width - 1)
    quarter = width // 4
    turns = (steps + quarter // 2) // quarter
    rest = (steps - turns * quarter).astype(F32) * (2.0 * math.pi / width)
    cosine, sine = sincos_small(rest)
    turns = turns & 3
    swap = (turns & 1) == 1
    first = jnp.where(swap, sine, cosine)
    second = jnp.where(swap, cosine, sine)
    first = jnp.where((turns == 1) | (turns == 2), -first, first)
    second = jnp.where(turns >= 2, -second, second)
    return first, second


def columns_mixed(pair, right_ref):
    high, low = halves(pair)
    return jnp.dot(
        jnp.concatenate([high, low, high], 1), right_ref[...], preferred_element_type=F32
    )


def rows_mixed(value, left_ref):
    high, low = halves(value)
    return jnp.dot(
        left_ref[...], jnp.concatenate([high, low, high], 0), preferred_element_type=F32
    )


def filtered(real, imag, mult_re, mult_im, left_ref, right_ref):
    width = real.shape[0]
    mixed = columns_mixed(jnp.concatenate([real, imag], 0), right_ref)
    real = rows_mixed(mixed[:width], left_ref)
    imag = rows_mixed(mixed[width:], left_ref)
    if mult_im is None:
        real, imag = real * mult_re, imag * mult_re
    else:
        real, imag = real * mult_re - imag * mult_im, real * mult_im + imag * mult_re
    real = rows_mixed(real, left_ref)
    imag = rows_mixed(imag, left_ref)
    mixed = columns_mixed(jnp.concatenate([real, imag], 0), right_ref)
    return mixed[:width], mixed[width:]


def kernel(
    pair_ref, cutoff_ref, index_ref, target_ref, left_ref, right_ref, wave_ref, square_ref,
    term_ref, field_ref, screen_ref, adjoint_ref,
):
    slices, width = index_ref.shape[0], index_ref.shape[1]
    kx, ky = pair_ref[0], pair_ref[1]
    whole = jnp.full((8, 128), kx * kx + ky * ky, jnp.int32).astype(F32)
    phi = 13.0 / width * (jnp.sqrt(0.64 * width * width - whole) - 0.8 * width)
    lead_re, lead_im = jnp.cos(phi)[:1, :1], jnp.sin(phi)[:1, :1]
    row_re, row_im = sincos_steps(
        kx * lax.broadcasted_iota(jnp.int32, (width, 1), 0), width
    )
    col_re, col_im = sincos_steps(
        ky * lax.broadcasted_iota(jnp.int32, (1, width), 1), width
    )
    row_re, row_im = row_re * lead_re - row_im * lead_im, row_re * lead_im + row_im * lead_re

    def screened(level, real, imag):
        screen_re, screen_im = sincos_small(screen_scale * index_ref[level])
        screen_ref[level, 0] = screen_re
        screen_ref[level, 1] = screen_im
        field_ref[level, 0] = real * screen_re - imag * screen_im
        field_ref[level, 1] = real * screen_im + imag * screen_re

    screened(0, row_re * col_re - row_im * col_im, row_re * col_im + row_im * col_re)

    def forward(level, carry):
        real, imag = filtered(
            field_ref[level - 1, 0], field_ref[level - 1, 1],
            wave_ref[0], wave_ref[1], left_ref, right_ref,
        )
        screened(level, real, imag)
        return carry

    lax.fori_loop(1, slices, forward, 0)
    cutoff = cutoff_ref[0]
    limit = (cutoff * cutoff).astype(F32)
    adjoint_ref[0] = field_ref[slices - 1, 0]
    adjoint_ref[1] = field_ref[slices - 1, 1]

    def through_pupil(turn, carry):
        pupil = (square_ref[...] <= limit).astype(F32)
        real, imag = filtered(
            adjoint_ref[0], adjoint_ref[1], pupil, None, left_ref, right_ref
        )
        misfit = 2.0 * (real * real + imag * imag - target_ref[...])
        misfit = jnp.where(turn == 0, misfit, 1.0)
        adjoint_ref[0] = misfit * real
        adjoint_ref[1] = misfit * imag
        return carry

    lax.fori_loop(0, 2, through_pupil, 0)

    def with_term(level):
        real, imag = adjoint_ref[0], adjoint_ref[1]
        term_ref[level] = screen_scale * (
            field_ref[level, 0] * imag - field_ref[level, 1] * real
        )
        return real, imag

    def backward(step, carry):
        level = slices - 1 - step
        real, imag = with_term(level)
        screen_re, screen_im = screen_ref[level, 0], screen_ref[level, 1]
        real, imag = real * screen_re + imag * screen_im, imag * screen_re - real * screen_im
        real, imag = filtered(
            real, imag, wave_ref[0], -wave_ref[1], left_ref, right_ref
        )
        adjoint_ref[0] = real
        adjoint_ref[1] = imag
        return carry

    lax.fori_loop(0, slices - 1, backward, 0)
    with_term(0)


def body(index_change, measured, angle_index, cutoff):
    width = index_change.shape[1]
    members = measured.shape[0]
    place = lax.axis_index("depth")
    whole = lax.all_gather(index_change, "depth", axis=0, tiled=True)
    slices = whole.shape[0]
    member = place % members
    target = lax.dynamic_index_in_dim(measured, member, 0, keepdims=False)
    pair = lax.dynamic_index_in_dim(angle_index, member, 0, keepdims=False)
    left, right, wave, square = tables(width)
    smem = pl.BlockSpec(memory_space=pltpu.SMEM)
    vmem = pl.BlockSpec(memory_space=pltpu.VMEM)
    terms = pl.pallas_call(
        kernel,
        out_shape=jax.ShapeDtypeStruct((slices, width, width), F32),
        in_specs=[smem] * 2 + [vmem] * 6,
        out_specs=vmem,
        scratch_shapes=[
            pltpu.VMEM((slices, 2, width, width), F32),
            pltpu.VMEM((slices, 2, width, width), F32),
            pltpu.VMEM((2, width, width), F32),
        ],
        compiler_params=pltpu.CompilerParams(vmem_limit_bytes=56 * 2**20),
    )(pair, cutoff, whole, target, left, right, wave, square)
    terms = jnp.where(place < members, terms, 0.0)
    terms = lax.psum_scatter(terms, "depth", scatter_dimension=0, tiled=True)
    return lax.psum_scatter(terms, "angle", scatter_dimension=1, tiled=True)


def solution(mesh):
    in_specs = (
        P(("blocks", "depth"), None, None),
        P(("blocks", "angle"), None, None),
        P(("blocks", "angle"), None),
        P(),
    )
    out_specs = P(("blocks", "depth"), "angle", None)
    return jax.shard_map(body, mesh=mesh, in_specs=in_specs, out_specs=out_specs, check_vma=False)
```

```python
import math

import jax
import jax.numpy as jnp
import numpy as np
from jax import lax
from jax.experimental import pallas as pl
from jax.experimental.pallas import tpu as pltpu
from jax.sharding import PartitionSpec as P

screen_scale = 0.25
F32 = jnp.float32
BF16 = jnp.bfloat16


def tables(width):
    index = np.arange(width)
    turn = 2.0 * np.pi / width * (index[:, None] * index[None, :] % width)
    hartley = ((np.cos(turn) + np.sin(turn)) / math.sqrt(width)).astype(np.float32)
    high = hartley.astype(BF16)
    low = (hartley - high.astype(np.float32)).astype(BF16)
    freq = (index + width // 2) % width - width // 2
    square = (freq[:, None] ** 2 + freq[None, :] ** 2).astype(np.float64)
    phi = 13.0 / width * (np.sqrt(0.64 * width * width - square) - 0.8 * width)
    wave = np.stack([np.cos(phi), np.sin(phi)]).astype(np.float32)
    return (
        np.concatenate([high, high, low], 1),
        np.concatenate([high, high, low], 0),
        wave,
        square.astype(np.float32),
    )


def halves(value):
    high = value.astype(BF16)
    return high, (value - high.astype(F32)).astype(BF16)


def sincos_small(angle):
    sq = angle * angle
    cosine = 1.0 + sq * (
        -0.5 + sq * (1 / 24 + sq * (-1 / 720 + sq * (1 / 40320 - sq * (1 / 3628800))))
    )
    sine = angle * (
        1.0 + sq * (-1 / 6 + sq * (1 / 120 + sq * (-1 / 5040 + sq * (1 / 362880))))
    )
    return cosine, sine


def sincos_steps(steps, width):
    steps = steps & (width - 1)
    quarter = width // 4
    turns = (steps + quarter // 2) // quarter
    rest = (steps - turns * quarter).astype(F32) * (2.0 * math.pi / width)
    cosine, sine = sincos_small(rest)
    turns = turns & 3
    swap = (turns & 1) == 1
    first = jnp.where(swap, sine, cosine)
    second = jnp.where(swap, cosine, sine)
    first = jnp.where((turns == 1) | (turns == 2), -first, first)
    second = jnp.where(turns >= 2, -second, second)
    return first, second


def columns_mixed(pair, right_ref):
    high, low = halves(pair)
    return jnp.dot(
        jnp.concatenate([high, low, high], 1), right_ref[...], preferred_element_type=F32
    )


def rows_mixed(value, left_ref):
    high, low = halves(value)
    return jnp.dot(
        left_ref[...], jnp.concatenate([high, low, high], 0), preferred_element_type=F32
    )


def filtered(real, imag, mult_re, mult_im, left_ref, right_ref):
    width = real.shape[0]
    mixed = columns_mixed(jnp.concatenate([real, imag], 0), right_ref)
    real = rows_mixed(mixed[:width], left_ref)
    imag = rows_mixed(mixed[width:], left_ref)
    if mult_im is None:
        real, imag = real * mult_re, imag * mult_re
    else:
        real, imag = real * mult_re - imag * mult_im, real * mult_im + imag * mult_re
    real = rows_mixed(real, left_ref)
    imag = rows_mixed(imag, left_ref)
    mixed = columns_mixed(jnp.concatenate([real, imag], 0), right_ref)
    return mixed[:width], mixed[width:]


MESH = pl.DeviceIdType.MESH


def kernel(
    pair_ref, cutoff_ref, index_ref, target_ref, left_ref, right_ref, wave_ref, square_ref,
    out_ref,
    gathered_ref, field_ref, adjoint_ref, term_ref, inbox_ref, total_ref, part_ref,
    own_send, relay_send, gather_recv, term_send, term_recv, sum_send, sum_recv,
    part_send, part_recv, turn_sem,
):
    slabs, width = index_ref.shape[0], index_ref.shape[1]
    slices = gathered_ref.shape[0]
    members = target_ref.shape[0]
    levels, angles = lax.axis_size("depth"), lax.axis_size("angle")
    rows = width // angles
    place, spoke = lax.axis_index("depth"), lax.axis_index("angle")
    worker = place < members

    barrier = pltpu.get_barrier_semaphore()
    for step in range(1, levels):
        pl.semaphore_signal(
            barrier, device_id={"depth": lax.rem(place + step, levels)}, device_id_type=MESH
        )
    for step in range(1, angles):
        pl.semaphore_signal(
            barrier, device_id={"angle": lax.rem(spoke + step, angles)}, device_id_type=MESH
        )
    pl.semaphore_wait(barrier, levels + angles - 2)

    def remote(source, target, send, recv, device):
        return pltpu.make_async_remote_copy(
            src_ref=source, dst_ref=target, send_sem=send, recv_sem=recv,
            device_id=device, device_id_type=MESH,
        )

    def own_copy(slab, step):
        level = place * slabs + slab
        return remote(
            index_ref.at[slab], gathered_ref.at[level], own_send.at[slab, step],
            gather_recv.at[level], {"depth": lax.rem(place + step, members)},
        )

    def relay_copy(level, step):
        return remote(
            gathered_ref.at[level], gathered_ref.at[level], relay_send.at[level, step],
            gather_recv.at[level], {"depth": lax.rem(place + step, members)},
        )

    def term_copy(level):
        entry = (level // slabs) % members
        slot = lax.rem(place - entry + members, members)
        return remote(
            term_ref.at[level], inbox_ref.at[level, slot], term_send.at[level],
            term_recv.at[level, slot], {"depth": entry},
        )

    def sum_copy(level):
        return remote(
            term_ref.at[level], total_ref.at[level % slabs], sum_send.at[level],
            sum_recv.at[level % slabs], {"depth": level // slabs},
        )

    def part_copy(slab, step):
        goal = lax.rem(spoke + step, angles)
        return remote(
            total_ref.at[slab, pl.ds(pl.multiple_of(goal * rows, rows), rows)],
            part_ref.at[slab, step], part_send.at[slab, step], part_recv.at[slab, step],
            {"angle": goal},
        )

    def start_parts(slab):
        for step in range(1, angles):
            part_copy(slab, step).start()

    @pl.when(jnp.logical_not(worker))
    def _():
        @pl.when(place > members)
        def _():
            pl.semaphore_wait(turn_sem, 1)

        for slab in range(slabs):
            copy = own_copy(slab, 0)
            copy.start()
            copy.wait_send()

        @pl.when(place < levels - 1)
        def _():
            pl.semaphore_signal(turn_sem, device_id={"depth": lax.rem(place + 1, levels)}, device_id_type=MESH)

        for slab in reversed(range(slabs)):
            sum_copy(place * slabs + slab).wait_recv()
            start_parts(slab)

    def work():
        kx, ky = pair_ref[place, 0], pair_ref[place, 1]
        whole = jnp.full((8, 128), kx * kx + ky * ky, jnp.int32).astype(F32)
        phi = 13.0 / width * (jnp.sqrt(0.64 * width * width - whole) - 0.8 * width)
        lead_re, lead_im = jnp.cos(phi)[:1, :1], jnp.sin(phi)[:1, :1]
        row_re, row_im = sincos_steps(
            kx * lax.broadcasted_iota(jnp.int32, (width, 1), 0), width
        )
        col_re, col_im = sincos_steps(
            ky * lax.broadcasted_iota(jnp.int32, (1, width), 1), width
        )
        row_re, row_im = row_re * lead_re - row_im * lead_im, row_re * lead_im + row_im * lead_re

        def relay(level):
            owner = level // slabs

            @pl.when((owner >= members) & (owner % members == place) & (level < slices))
            def _():
                relay_copy(level, 0).wait_recv()
                for step in range(1, members):
                    relay_copy(level, step).start()

        def ready(level):
            owner = level // slabs

            @pl.when((owner != place) & ((owner < members) | (owner % members != place)))
            def _():
                relay_copy(level, 0).wait_recv()

        def screened(level, real, imag):
            screen_re, screen_im = sincos_small(screen_scale * gathered_ref[level])
            field_ref[level, 0] = real * screen_re - imag * screen_im
            field_ref[level, 1] = real * screen_im + imag * screen_re

        relay(0)
        relay(1)
        ready(0)
        screened(0, row_re * col_re - row_im * col_im, row_re * col_im + row_im * col_re)

        def forward(level, carry):
            real, imag = filtered(
                field_ref[level - 1, 0], field_ref[level - 1, 1],
                wave_ref[0], wave_ref[1], left_ref, right_ref,
            )
            relay(level + 1)
            ready(level)
            screened(level, real, imag)
            return carry

        lax.fori_loop(1, slices, forward, 0)
        cutoff = cutoff_ref[0]
        limit = (cutoff * cutoff).astype(F32)
        adjoint_ref[0] = field_ref[slices - 1, 0]
        adjoint_ref[1] = field_ref[slices - 1, 1]

        def through_pupil(turn, carry):
            pupil = (square_ref[...] <= limit).astype(F32)
            real, imag = filtered(
                adjoint_ref[0], adjoint_ref[1], pupil, None, left_ref, right_ref
            )
            misfit = 2.0 * (real * real + imag * imag - target_ref[place])
            misfit = jnp.where(turn == 0, misfit, 1.0)
            adjoint_ref[0] = misfit * real
            adjoint_ref[1] = misfit * imag
            return carry

        lax.fori_loop(0, 2, through_pupil, 0)

        def with_term(level):
            real, imag = adjoint_ref[0], adjoint_ref[1]
            term_ref[level] = screen_scale * (
                field_ref[level, 0] * imag - field_ref[level, 1] * real
            )

            @pl.when((level // slabs) % members != place)
            def _():
                term_copy(level).start()

            return real, imag

        def pass_on(level):
            owner = level // slabs

            @pl.when(owner % members == place)
            def _():
                value = term_ref[level]
                for slot in range(1, members):
                    remote(
                        inbox_ref.at[level, slot], inbox_ref.at[level, slot],
                        term_send.at[level], term_recv.at[level, slot], {"depth": lax.rem(place + 1, levels)},
                    ).wait_recv()
                    value = value + inbox_ref[level, slot]

                @pl.when(owner == place)
                def _():
                    total_ref[level % slabs] = value
                    start_parts(level % slabs)

                @pl.when(owner != place)
                def _():
                    term_ref[level] = value
                    sum_copy(level).start()

        def backward(step, carry):
            level = slices - 1 - step
            real, imag = with_term(level)
            screen_re, screen_im = sincos_small(screen_scale * gathered_ref[level])
            real, imag = real * screen_re + imag * screen_im, imag * screen_re - real * screen_im
            real, imag = filtered(
                real, imag, wave_ref[0], -wave_ref[1], left_ref, right_ref
            )
            adjoint_ref[0] = real
            adjoint_ref[1] = imag
            pass_on(level)
            return carry

        lax.fori_loop(0, slices - 1, backward, 0)
        with_term(0)
        pass_on(0)

    @pl.when(worker)
    def _():
        for slab in range(slabs):
            for step in range(1, members):
                own_copy(slab, step).start()
        for slab in range(slabs):
            gathered_ref[place * slabs + slab] = index_ref[slab]
        work()

    for slab in reversed(range(slabs)):
        value = total_ref[slab, pl.ds(pl.multiple_of(spoke * rows, rows), rows)]
        for step in range(1, angles):
            part_copy(slab, step).wait_recv()
            value = value + part_ref[slab, step]
        out_ref[slab] = value

    for slab in range(slabs):
        for step in range(1, angles):
            part_copy(slab, step).wait_send()

    @pl.when(worker)
    def _():
        for slab in range(slabs):
            for step in range(1, members):
                own_copy(slab, step).wait_send()

        def finish(level, carry):
            owner = level // slabs
            entry = owner % members

            @pl.when((owner >= members) & (entry == place))
            def _():
                for step in range(1, members):
                    relay_copy(level, step).wait_send()
                sum_copy(level).wait_send()

            @pl.when(entry != place)
            def _():
                term_copy(level).wait_send()

            return carry

        lax.fori_loop(0, slices, finish, 0)


def body(index_change, measured, angle_index, cutoff):
    slabs, width = index_change.shape[0], index_change.shape[1]
    members = measured.shape[0]
    levels, angles = lax.axis_size("depth"), lax.axis_size("angle")
    slices = slabs * levels
    left, right, wave, square = tables(width)
    smem = pl.BlockSpec(memory_space=pltpu.SMEM)
    vmem = pl.BlockSpec(memory_space=pltpu.VMEM)
    sem = pltpu.SemaphoreType.DMA
    return pl.pallas_call(
        kernel,
        out_shape=jax.ShapeDtypeStruct((slabs, width // angles, width), F32),
        in_specs=[smem] * 2 + [vmem] * 6,
        out_specs=vmem,
        scratch_shapes=[
            pltpu.VMEM((slices, width, width), F32),
            pltpu.VMEM((slices, 2, width, width), F32),
            pltpu.VMEM((2, width, width), F32),
            pltpu.VMEM((slices, width, width), F32),
            pltpu.VMEM((slices, members, width, width), F32),
            pltpu.VMEM((slabs, width, width), F32),
            pltpu.VMEM((slabs, angles, width // angles, width), F32),
            sem((slabs, members)),
            sem((slices, members)),
            sem((slices,)),
            sem((slices,)),
            sem((slices, members)),
            sem((slices,)),
            sem((slabs,)),
            sem((slabs, angles)),
            sem((slabs, angles)),
            pltpu.SemaphoreType.REGULAR,
        ],
        compiler_params=pltpu.CompilerParams(
            collective_id=0, has_side_effects=True, vmem_limit_bytes=60 * 2**20
        ),
    )(angle_index, cutoff, index_change, measured, left, right, wave, square)


def solution(mesh):
    in_specs = (
        P(("blocks", "depth"), None, None),
        P(("blocks", "angle"), None, None),
        P(("blocks", "angle"), None),
        P(),
    )
    out_specs = P(("blocks", "depth"), "angle", None)
    return jax.shard_map(body, mesh=mesh, in_specs=in_specs, out_specs=out_specs, check_vma=False)
```

```python
import math

import jax
import jax.numpy as jnp
import numpy as np
from jax import lax
from jax.experimental import pallas as pl
from jax.experimental.pallas import tpu as pltpu
from jax.sharding import PartitionSpec as P

screen_scale = 0.25
F32 = jnp.float32
BF16 = jnp.bfloat16


def tables(width):
    index = np.arange(width)
    turn = 2.0 * np.pi / width * (index[:, None] * index[None, :] % width)
    hartley = ((np.cos(turn) + np.sin(turn)) / math.sqrt(width)).astype(np.float32)
    high = hartley.astype(BF16)
    low = (hartley - high.astype(np.float32)).astype(BF16)
    freq = (index + width // 2) % width - width // 2
    square = (freq[:, None] ** 2 + freq[None, :] ** 2).astype(np.float64)
    phi = 13.0 / width * (np.sqrt(0.64 * width * width - square) - 0.8 * width)
    wave = np.stack([np.cos(phi), np.sin(phi)]).astype(np.float32)
    return np.stack([high, low]), wave


def halves(value):
    high = value.astype(BF16)
    return high, (value - high.astype(F32)).astype(BF16)


def sincos_small(angle):
    sq = angle * angle
    cosine = 1.0 + sq * (
        -0.5 + sq * (1 / 24 + sq * (-1 / 720 + sq * (1 / 40320 - sq * (1 / 3628800))))
    )
    sine = angle * (
        1.0 + sq * (-1 / 6 + sq * (1 / 120 + sq * (-1 / 5040 + sq * (1 / 362880))))
    )
    return cosine, sine


def sincos_steps(steps, width):
    steps = steps & (width - 1)
    quarter = width // 4
    turns = (steps + quarter // 2) // quarter
    rest = (steps - turns * quarter).astype(F32) * (2.0 * math.pi / width)
    cosine, sine = sincos_small(rest)
    turns = turns & 3
    swap = (turns & 1) == 1
    first = jnp.where(swap, sine, cosine)
    second = jnp.where(swap, cosine, sine)
    first = jnp.where((turns == 1) | (turns == 2), -first, first)
    second = jnp.where(turns >= 2, -second, second)
    return first, second


def columns_mixed(pair, mix_ref):
    high, low = halves(pair)
    return (
        jnp.dot(high, mix_ref[0], preferred_element_type=F32)
        + jnp.dot(low, mix_ref[0], preferred_element_type=F32)
        + jnp.dot(high, mix_ref[1], preferred_element_type=F32)
    )


def rows_mixed(value, mix_ref):
    high, low = halves(value)
    return (
        jnp.dot(mix_ref[0], high, preferred_element_type=F32)
        + jnp.dot(mix_ref[0], low, preferred_element_type=F32)
        + jnp.dot(mix_ref[1], high, preferred_element_type=F32)
    )


def filtered(real, imag, mult_re, mult_im, mix_ref):
    width = real.shape[0]
    mixed = columns_mixed(jnp.concatenate([real, imag], 0), mix_ref)
    real = rows_mixed(mixed[:width], mix_ref)
    imag = rows_mixed(mixed[width:], mix_ref)
    if mult_im is None:
        real, imag = real * mult_re, imag * mult_re
    else:
        real, imag = real * mult_re - imag * mult_im, real * mult_im + imag * mult_re
    real = rows_mixed(real, mix_ref)
    imag = rows_mixed(imag, mix_ref)
    mixed = columns_mixed(jnp.concatenate([real, imag], 0), mix_ref)
    return mixed[:width], mixed[width:]


MESH = pl.DeviceIdType.MESH


def kernel(
    pair_ref, cutoff_ref, index_hbm, target_hbm, mix_hbm, wave_hbm,
    out_ref,
    target_ref, mix_ref, wave_ref, gathered_ref, field_ref, adjoint_ref, square_ref, term_ref, inbox_ref, total_ref, part_ref,
    own_send, relay_send, gather_recv, term_send, term_recv, sum_send, sum_recv,
    part_send, part_recv, load_sem,
):
    slabs, width = index_hbm.shape[0], index_hbm.shape[1]
    slices = gathered_ref.shape[0]
    members = target_hbm.shape[0]
    levels, angles = lax.axis_size("depth"), lax.axis_size("angle")
    rows = width // angles
    place, spoke = lax.axis_index("depth"), lax.axis_index("angle")
    worker = place < members
    pieces = 2 - angles % 2
    piece = spoke % pieces
    partner = spoke + 1 - 2 * piece if pieces == 2 else spoke

    def load(number):
        pairs = (
            (mix_hbm, mix_ref),
            (wave_hbm, wave_ref),
            (target_hbm.at[lax.rem(place, members)], target_ref),
        )
        return pltpu.make_async_copy(*pairs[number], load_sem.at[slabs + number])

    def load_slab(slab):
        return pltpu.make_async_copy(
            index_hbm.at[slab], gathered_ref.at[place * slabs + slab], load_sem.at[slab]
        )

    for slab in range(slabs):
        load_slab(slab).start()

    @pl.when(worker)
    def _():
        for number in range(3):
            load(number).start()

    barrier = pltpu.get_barrier_semaphore()
    for step in range(1, levels):
        pl.semaphore_signal(
            barrier, device_id={"depth": lax.rem(place + step, levels)}, device_id_type=MESH
        )
    for step in range(1, angles):
        pl.semaphore_signal(
            barrier, device_id={"angle": lax.rem(spoke + step, angles)}, device_id_type=MESH
        )
    if pieces == 2:
        @pl.when(worker)
        def _():
            for step in range(1, members):
                pl.semaphore_signal(
                    barrier,
                    device_id={"depth": lax.rem(place + step, members), "angle": partner},
                    device_id_type=MESH,
                )
            pl.semaphore_wait(barrier, levels + angles + members - 3)

        @pl.when(jnp.logical_not(worker))
        def _():
            pl.semaphore_wait(barrier, levels + angles - 2)
    else:
        pl.semaphore_wait(barrier, levels + angles - 2)

    def remote(source, target, send, recv, device):
        return pltpu.make_async_remote_copy(
            src_ref=source, dst_ref=target, send_sem=send, recv_sem=recv,
            device_id=device, device_id_type=MESH,
        )

    tall = width // pieces

    def piece_of(level, number):
        return gathered_ref.at[level, pl.ds(pl.multiple_of(number * tall, tall), tall)]

    def own_copy(slab, step):
        level = place * slabs + slab
        return remote(
            gathered_ref.at[level], gathered_ref.at[level], own_send.at[slab, step],
            gather_recv.at[level, 0], {"depth": lax.rem(place + step, members)},
        )

    def own_wait(level):
        remote(
            gathered_ref.at[level], gathered_ref.at[level], relay_send.at[level, 0, 0],
            gather_recv.at[level, 0], {"depth": lax.rem(place + 1, levels)},
        ).wait_recv()

    def entry_copy(slab):
        level = place * slabs + slab
        return remote(
            piece_of(level, piece), piece_of(level, piece), own_send.at[slab, 0],
            gather_recv.at[level, piece], {"depth": lax.rem(place, members)},
        )

    def relay_copy(level, step, across):
        device = {"depth": lax.rem(place + step, members)}
        if across:
            device["angle"] = partner
        return remote(
            piece_of(level, piece), piece_of(level, piece),
            relay_send.at[level, across, step], gather_recv.at[level, piece], device,
        )

    relays = [(step, across) for across in range(pieces) for step in range(members) if step + across]

    def piece_wait(level, number):
        remote(
            piece_of(level, number), piece_of(level, number), relay_send.at[level, 0, 0],
            gather_recv.at[level, number], {"depth": lax.rem(place + 1, levels)},
        ).wait_recv()

    def term_copy(level):
        entry = (level // slabs) % members
        slot = lax.rem(place - entry + members, members)
        return remote(
            term_ref.at[level], inbox_ref.at[level, slot], term_send.at[level],
            term_recv.at[level, slot], {"depth": entry},
        )

    def sum_copy(level):
        return remote(
            term_ref.at[level], total_ref.at[level % slabs], sum_send.at[level],
            sum_recv.at[level % slabs], {"depth": level // slabs},
        )

    def part_copy(slab, step):
        goal = lax.rem(spoke + step, angles)
        return remote(
            total_ref.at[slab, pl.ds(pl.multiple_of(goal * rows, rows), rows)],
            part_ref.at[slab, step], part_send.at[slab, step], part_recv.at[slab, step],
            {"angle": goal},
        )

    def start_parts(slab):
        for step in range(1, angles):
            part_copy(slab, step).start()

    @pl.when(jnp.logical_not(worker))
    def _():
        for slab in range(slabs):
            load_slab(slab).wait()
            entry_copy(slab).start()

        for slab in reversed(range(slabs)):
            sum_copy(place * slabs + slab).wait_recv()
            start_parts(slab)

        for slab in range(slabs):
            entry_copy(slab).wait_send()

    def work():
        kx, ky = pair_ref[place, 0], pair_ref[place, 1]
        whole = jnp.full((8, 128), kx * kx + ky * ky, jnp.int32).astype(F32)
        phi = 13.0 / width * (jnp.sqrt(0.64 * width * width - whole) - 0.8 * width)
        lead_re, lead_im = jnp.cos(phi)[:1, :1], jnp.sin(phi)[:1, :1]
        row_re, row_im = sincos_steps(
            kx * lax.broadcasted_iota(jnp.int32, (width, 1), 0), width
        )
        col_re, col_im = sincos_steps(
            ky * lax.broadcasted_iota(jnp.int32, (1, width), 1), width
        )
        row_re, row_im = row_re * lead_re - row_im * lead_im, row_re * lead_im + row_im * lead_re

        def frequency(index):
            return jnp.where(index < width // 2, index, index - width)

        def relay(level):
            owner = level // slabs

            @pl.when((owner >= members) & (owner % members == place) & (level < slices))
            def _():
                piece_wait(level, piece)
                for step, across in relays:
                    relay_copy(level, step, across).start()

        def ready(level):
            owner = level // slabs

            @pl.when((owner != place) & (owner < members))
            def _():
                own_wait(level)

            @pl.when((owner >= members) & (owner % members != place))
            def _():
                piece_wait(level, piece)

            if pieces == 2:
                @pl.when(owner >= members)
                def _():
                    piece_wait(level, 1 - piece)

        def screened(level, real, imag):
            screen_re, screen_im = sincos_small(screen_scale * gathered_ref[level])
            field_ref[level, 0] = real * screen_re - imag * screen_im
            field_ref[level, 1] = real * screen_im + imag * screen_re

        relay(0)
        relay(1)
        relay(2)
        ready(0)
        screened(0, row_re * col_re - row_im * col_im, row_re * col_im + row_im * col_re)

        def forward(level, carry):
            real, imag = filtered(
                field_ref[level - 1, 0], field_ref[level - 1, 1],
                wave_ref[0], wave_ref[1], mix_ref,
            )
            relay(level + 2)
            ready(level)
            screened(level, real, imag)
            return carry

        for number in range(2):
            load(number).wait()
        lax.fori_loop(1, slices, forward, 0)
        load(2).wait()
        freq_row = frequency(lax.broadcasted_iota(jnp.int32, (width, width), 0))
        freq_col = frequency(lax.broadcasted_iota(jnp.int32, (width, width), 1))
        square_ref[...] = (freq_row * freq_row + freq_col * freq_col).astype(F32)
        cutoff = cutoff_ref[0]
        limit = (cutoff * cutoff).astype(F32)
        adjoint_ref[0] = field_ref[slices - 1, 0]
        adjoint_ref[1] = field_ref[slices - 1, 1]

        def through_pupil(turn, carry):
            pupil = (square_ref[...] <= limit).astype(F32)
            real, imag = filtered(
                adjoint_ref[0], adjoint_ref[1], pupil, None, mix_ref
            )
            misfit = 2.0 * (real * real + imag * imag - target_ref[...])
            misfit = jnp.where(turn == 0, misfit, 1.0)
            adjoint_ref[0] = misfit * real
            adjoint_ref[1] = misfit * imag
            return carry

        lax.fori_loop(0, 2, through_pupil, 0)

        def with_term(level):
            real, imag = adjoint_ref[0], adjoint_ref[1]
            term_ref[level] = screen_scale * (
                field_ref[level, 0] * imag - field_ref[level, 1] * real
            )

            @pl.when((level // slabs) % members != place)
            def _():
                term_copy(level).start()

            return real, imag

        def pass_on(level):
            owner = level // slabs

            @pl.when(owner % members == place)
            def _():
                value = term_ref[level]
                for slot in range(1, members):
                    remote(
                        inbox_ref.at[level, slot], inbox_ref.at[level, slot],
                        term_send.at[level], term_recv.at[level, slot], {"depth": lax.rem(place + 1, levels)},
                    ).wait_recv()
                    value = value + inbox_ref[level, slot]

                @pl.when(owner == place)
                def _():
                    total_ref[level % slabs] = value
                    start_parts(level % slabs)

                @pl.when(owner != place)
                def _():
                    term_ref[level] = value
                    sum_copy(level).start()

        def backward(step, carry):
            level = slices - 1 - step
            real, imag = with_term(level)
            screen_re, screen_im = sincos_small(screen_scale * gathered_ref[level])
            real, imag = real * screen_re + imag * screen_im, imag * screen_re - real * screen_im
            real, imag = filtered(
                real, imag, wave_ref[0], -wave_ref[1], mix_ref
            )
            adjoint_ref[0] = real
            adjoint_ref[1] = imag
            pass_on(level)
            return carry

        lax.fori_loop(0, slices - 1, backward, 0)
        with_term(0)
        pass_on(0)

    @pl.when(worker)
    def _():
        for slab in range(slabs):
            load_slab(slab).wait()
            for step in range(1, members):
                own_copy(slab, step).start()
        work()

    for slab in reversed(range(slabs)):
        value = total_ref[slab, pl.ds(pl.multiple_of(spoke * rows, rows), rows)]
        for step in range(1, angles):
            part_copy(slab, step).wait_recv()
            value = value + part_ref[slab, step]
        out_ref[slab] = value

    for slab in range(slabs):
        for step in range(1, angles):
            part_copy(slab, step).wait_send()

    @pl.when(worker)
    def _():
        for slab in range(slabs):
            for step in range(1, members):
                own_copy(slab, step).wait_send()

        def finish(level, carry):
            owner = level // slabs
            entry = owner % members

            @pl.when((owner >= members) & (entry == place))
            def _():
                for step, across in relays:
                    relay_copy(level, step, across).wait_send()
                sum_copy(level).wait_send()

            @pl.when(entry != place)
            def _():
                term_copy(level).wait_send()

            return carry

        lax.fori_loop(0, slices, finish, 0)


def body(index_change, measured, angle_index, cutoff):
    slabs, width = index_change.shape[0], index_change.shape[1]
    members = measured.shape[0]
    levels, angles = lax.axis_size("depth"), lax.axis_size("angle")
    slices = slabs * levels
    mix, wave = tables(width)
    smem = pl.BlockSpec(memory_space=pltpu.SMEM)
    hbm = pl.BlockSpec(memory_space=pl.ANY)
    sem = pltpu.SemaphoreType.DMA
    return pl.pallas_call(
        kernel,
        out_shape=jax.ShapeDtypeStruct((slabs, width // angles, width), F32),
        in_specs=[smem] * 2 + [hbm] * 4,
        out_specs=pl.BlockSpec(memory_space=pltpu.VMEM),
        scratch_shapes=[
            pltpu.VMEM((width, width), F32),
            pltpu.VMEM((2, width, width), BF16),
            pltpu.VMEM((2, width, width), F32),
            pltpu.VMEM((slices, width, width), F32),
            pltpu.VMEM((slices, 2, width, width), F32),
            pltpu.VMEM((2, width, width), F32),
            pltpu.VMEM((width, width), F32),
            pltpu.VMEM((slices, width, width), F32),
            pltpu.VMEM((slices, members, width, width), F32),
            pltpu.VMEM((slabs, width, width), F32),
            pltpu.VMEM((slabs, angles, width // angles, width), F32),
            sem((slabs, members)),
            sem((slices, 2, members)),
            sem((slices, 2)),
            sem((slices,)),
            sem((slices, members)),
            sem((slices,)),
            sem((slabs,)),
            sem((slabs, angles)),
            sem((slabs, angles)),
            sem((slabs + 3,)),
        ],
        compiler_params=pltpu.CompilerParams(
            collective_id=0, has_side_effects=True, vmem_limit_bytes=60 * 2**20
        ),
    )(angle_index, cutoff, index_change, measured, mix, wave)


def solution(mesh):
    in_specs = (
        P(("blocks", "depth"), None, None),
        P(("blocks", "angle"), None, None),
        P(("blocks", "angle"), None),
        P(),
    )
    out_specs = P(("blocks", "depth"), "angle", None)
    return jax.shard_map(body, mesh=mesh, in_specs=in_specs, out_specs=out_specs, check_vma=False)
```

```python
import math

import jax
import jax.numpy as jnp
import numpy as np
from jax import lax
from jax.experimental import pallas as pl
from jax.experimental.pallas import tpu as pltpu
from jax.sharding import PartitionSpec as P

screen_scale = 0.25
F32 = jnp.float32
BF16 = jnp.bfloat16


def tables(width):
    index = np.arange(width)
    turn = 2.0 * np.pi / width * (index[:, None] * index[None, :] % width)
    hartley = ((np.cos(turn) + np.sin(turn)) / math.sqrt(width)).astype(np.float32)
    high = hartley.astype(BF16)
    low = (hartley - high.astype(np.float32)).astype(BF16)
    freq = (index + width // 2) % width - width // 2
    square = (freq[:, None] ** 2 + freq[None, :] ** 2).astype(np.float64)
    phi = 13.0 / width * (np.sqrt(0.64 * width * width - square) - 0.8 * width)
    wave = np.stack([np.cos(phi), np.sin(phi)]).astype(np.float32)
    return np.stack([high, low]), wave


def halves(value):
    high = value.astype(BF16)
    return high, (value - high.astype(F32)).astype(BF16)


def sincos_small(angle):
    sq = angle * angle
    cosine = 1.0 + sq * (
        -0.5 + sq * (1 / 24 + sq * (-1 / 720 + sq * (1 / 40320 - sq * (1 / 3628800))))
    )
    sine = angle * (
        1.0 + sq * (-1 / 6 + sq * (1 / 120 + sq * (-1 / 5040 + sq * (1 / 362880))))
    )
    return cosine, sine


def sincos_steps(steps, width):
    steps = steps & (width - 1)
    quarter = width // 4
    turns = (steps + quarter // 2) // quarter
    rest = (steps - turns * quarter).astype(F32) * (2.0 * math.pi / width)
    cosine, sine = sincos_small(rest)
    turns = turns & 3
    swap = (turns & 1) == 1
    first = jnp.where(swap, sine, cosine)
    second = jnp.where(swap, cosine, sine)
    first = jnp.where((turns == 1) | (turns == 2), -first, first)
    second = jnp.where(turns >= 2, -second, second)
    return first, second


def columns_mixed(pair, mix_ref):
    high, low = halves(pair)
    return (
        jnp.dot(high, mix_ref[0], preferred_element_type=F32)
        + jnp.dot(low, mix_ref[0], preferred_element_type=F32)
        + jnp.dot(high, mix_ref[1], preferred_element_type=F32)
    )


def rows_mixed(value, mix_ref):
    high, low = halves(value)
    return (
        jnp.dot(mix_ref[0], high, preferred_element_type=F32)
        + jnp.dot(mix_ref[0], low, preferred_element_type=F32)
        + jnp.dot(mix_ref[1], high, preferred_element_type=F32)
    )


def filtered(real, imag, mult_re, mult_im, mix_ref):
    width = real.shape[0]
    mixed = columns_mixed(jnp.concatenate([real, imag], 0), mix_ref)
    real = rows_mixed(mixed[:width], mix_ref)
    imag = rows_mixed(mixed[width:], mix_ref)
    if mult_im is None:
        real, imag = real * mult_re, imag * mult_re
    else:
        real, imag = real * mult_re - imag * mult_im, real * mult_im + imag * mult_re
    real = rows_mixed(real, mix_ref)
    imag = rows_mixed(imag, mix_ref)
    mixed = columns_mixed(jnp.concatenate([real, imag], 0), mix_ref)
    return mixed[:width], mixed[width:]


MESH = pl.DeviceIdType.MESH


def kernel(
    pair_ref, cutoff_ref, index_hbm, target_hbm, mix_hbm, wave_hbm,
    out_ref,
    target_ref, mix_ref, wave_ref, gathered_ref, field_ref, adjoint_ref, square_ref, term_ref, inbox_ref, total_ref, part_ref,
    own_send, relay_send, gather_recv, term_send, term_recv, sum_send, sum_recv,
    part_send, part_recv, load_sem, turn_sem,
):
    slabs, width = index_hbm.shape[0], index_hbm.shape[1]
    slices = gathered_ref.shape[0]
    members = target_hbm.shape[0]
    levels, angles = lax.axis_size("depth"), lax.axis_size("angle")
    rows = width // angles
    place, spoke = lax.axis_index("depth"), lax.axis_index("angle")
    worker = place < members
    pieces = 2 - angles % 2
    piece = spoke % pieces
    partner = spoke + 1 - 2 * piece if pieces == 2 else spoke

    def load(number):
        pairs = (
            (mix_hbm, mix_ref),
            (wave_hbm, wave_ref),
            (target_hbm.at[lax.rem(place, members)], target_ref),
        )
        return pltpu.make_async_copy(*pairs[number], load_sem.at[slabs + number])

    def load_slab(slab):
        return pltpu.make_async_copy(
            index_hbm.at[slab], gathered_ref.at[place * slabs + slab], load_sem.at[slab]
        )

    for slab in range(slabs):
        load_slab(slab).start()

    @pl.when(worker)
    def _():
        for number in range(3):
            load(number).start()

    barrier = pltpu.get_barrier_semaphore()
    for step in range(1, levels):
        pl.semaphore_signal(
            barrier, device_id={"depth": lax.rem(place + step, levels)}, device_id_type=MESH
        )
    for step in range(1, angles):
        pl.semaphore_signal(
            barrier, device_id={"angle": lax.rem(spoke + step, angles)}, device_id_type=MESH
        )
    pl.semaphore_wait(barrier, levels + angles - 2)

    def remote(source, target, send, recv, device):
        return pltpu.make_async_remote_copy(
            src_ref=source, dst_ref=target, send_sem=send, recv_sem=recv,
            device_id=device, device_id_type=MESH,
        )

    tall = width // pieces

    def piece_of(level, number):
        return gathered_ref.at[level, pl.ds(pl.multiple_of(number * tall, tall), tall)]

    def own_copy(slab, step):
        level = place * slabs + slab
        return remote(
            gathered_ref.at[level], gathered_ref.at[level], own_send.at[slab, step],
            gather_recv.at[level, 0], {"depth": lax.rem(place + step, members)},
        )

    def own_wait(level):
        remote(
            gathered_ref.at[level], gathered_ref.at[level], relay_send.at[level, 0, 0],
            gather_recv.at[level, 0], {"depth": lax.rem(place + 1, levels)},
        ).wait_recv()

    def entry_copy(slab):
        level = place * slabs + slab
        return remote(
            piece_of(level, piece), piece_of(level, piece), own_send.at[slab, 0],
            gather_recv.at[level, piece], {"depth": lax.rem(place, members)},
        )

    def relay_copy(level, number, step):
        return remote(
            piece_of(level, number), piece_of(level, number),
            relay_send.at[level, number, step], gather_recv.at[level, number],
            {"depth": lax.rem(place + step, members)},
        )

    def cross_copy(level):
        return remote(
            piece_of(level, piece), piece_of(level, piece),
            relay_send.at[level, 0, 0], gather_recv.at[level, piece], {"angle": partner},
        )

    def piece_wait(level, number):
        remote(
            piece_of(level, number), piece_of(level, number), relay_send.at[level, 0, 0],
            gather_recv.at[level, number], {"depth": lax.rem(place + 1, levels)},
        ).wait_recv()

    def term_copy(level):
        entry = (level // slabs) % members
        slot = lax.rem(place - entry + members, members)
        return remote(
            term_ref.at[level], inbox_ref.at[level, slot], term_send.at[level],
            term_recv.at[level, slot], {"depth": entry},
        )

    def sum_copy(level):
        return remote(
            term_ref.at[level], total_ref.at[level % slabs], sum_send.at[level],
            sum_recv.at[level % slabs], {"depth": level // slabs},
        )

    def part_copy(slab, step):
        goal = lax.rem(spoke + step, angles)
        return remote(
            total_ref.at[slab, pl.ds(pl.multiple_of(goal * rows, rows), rows)],
            part_ref.at[slab, step], part_send.at[slab, step], part_recv.at[slab, step],
            {"angle": goal},
        )

    def start_parts(slab):
        for step in range(1, angles):
            part_copy(slab, step).start()

    @pl.when(jnp.logical_not(worker))
    def _():
        for slab in range(slabs):
            load_slab(slab).wait()

        @pl.when(place > members)
        def _():
            pl.semaphore_wait(turn_sem, 1)

        for slab in range(slabs):
            entry_copy(slab).start()
        for slab in range(slabs):
            entry_copy(slab).wait_send()

        @pl.when(place < levels - 1)
        def _():
            pl.semaphore_signal(
                turn_sem, device_id={"depth": lax.rem(place + 1, levels)}, device_id_type=MESH
            )

        for slab in reversed(range(slabs)):
            sum_copy(place * slabs + slab).wait_recv()
            start_parts(slab)

    def work():
        kx, ky = pair_ref[place, 0], pair_ref[place, 1]
        whole = jnp.full((8, 128), kx * kx + ky * ky, jnp.int32).astype(F32)
        phi = 13.0 / width * (jnp.sqrt(0.64 * width * width - whole) - 0.8 * width)
        lead_re, lead_im = jnp.cos(phi)[:1, :1], jnp.sin(phi)[:1, :1]
        row_re, row_im = sincos_steps(
            kx * lax.broadcasted_iota(jnp.int32, (width, 1), 0), width
        )
        col_re, col_im = sincos_steps(
            ky * lax.broadcasted_iota(jnp.int32, (1, width), 1), width
        )
        row_re, row_im = row_re * lead_re - row_im * lead_im, row_re * lead_im + row_im * lead_re

        def frequency(index):
            return jnp.where(index < width // 2, index, index - width)

        def relay(level):
            owner = level // slabs

            @pl.when((owner >= members) & (owner % members == place) & (level < slices))
            def _():
                piece_wait(level, piece)
                if pieces == 2:
                    cross_copy(level).start()
                for step in range(1, members):
                    relay_copy(level, piece, step).start()

        def second_relay(level):
            owner = level // slabs

            if pieces == 2:
                @pl.when((owner >= members) & (owner % members == place) & (level < slices))
                def _():
                    piece_wait(level, 1 - piece)
                    for step in range(1, members):
                        relay_copy(level, 1 - piece, step).start()

        def ready(level):
            owner = level // slabs

            @pl.when((owner != place) & (owner < members))
            def _():
                own_wait(level)

            @pl.when((owner >= members) & (owner % members != place))
            def _():
                for number in range(pieces):
                    piece_wait(level, number)

        def screened(level, real, imag):
            screen_re, screen_im = sincos_small(screen_scale * gathered_ref[level])
            field_ref[level, 0] = real * screen_re - imag * screen_im
            field_ref[level, 1] = real * screen_im + imag * screen_re

        relay(0)
        relay(1)
        relay(2)
        second_relay(0)
        second_relay(1)
        ready(0)
        screened(0, row_re * col_re - row_im * col_im, row_re * col_im + row_im * col_re)

        def forward(level, carry):
            real, imag = filtered(
                field_ref[level - 1, 0], field_ref[level - 1, 1],
                wave_ref[0], wave_ref[1], mix_ref,
            )
            relay(level + 2)
            second_relay(level + 1)
            ready(level)
            screened(level, real, imag)
            return carry

        for number in range(2):
            load(number).wait()
        lax.fori_loop(1, slices, forward, 0)
        load(2).wait()
        freq_row = frequency(lax.broadcasted_iota(jnp.int32, (width, width), 0))
        freq_col = frequency(lax.broadcasted_iota(jnp.int32, (width, width), 1))
        square_ref[...] = (freq_row * freq_row + freq_col * freq_col).astype(F32)
        cutoff = cutoff_ref[0]
        limit = (cutoff * cutoff).astype(F32)
        adjoint_ref[0] = field_ref[slices - 1, 0]
        adjoint_ref[1] = field_ref[slices - 1, 1]

        def through_pupil(turn, carry):
            pupil = (square_ref[...] <= limit).astype(F32)
            real, imag = filtered(
                adjoint_ref[0], adjoint_ref[1], pupil, None, mix_ref
            )
            misfit = 2.0 * (real * real + imag * imag - target_ref[...])
            misfit = jnp.where(turn == 0, misfit, 1.0)
            adjoint_ref[0] = misfit * real
            adjoint_ref[1] = misfit * imag
            return carry

        lax.fori_loop(0, 2, through_pupil, 0)

        def with_term(level):
            real, imag = adjoint_ref[0], adjoint_ref[1]
            term_ref[level] = screen_scale * (
                field_ref[level, 0] * imag - field_ref[level, 1] * real
            )

            @pl.when((level // slabs) % members != place)
            def _():
                term_copy(level).start()

            return real, imag

        def pass_on(level):
            owner = level // slabs

            @pl.when(owner % members == place)
            def _():
                value = term_ref[level]
                for slot in range(1, members):
                    remote(
                        inbox_ref.at[level, slot], inbox_ref.at[level, slot],
                        term_send.at[level], term_recv.at[level, slot], {"depth": lax.rem(place + 1, levels)},
                    ).wait_recv()
                    value = value + inbox_ref[level, slot]

                @pl.when(owner == place)
                def _():
                    total_ref[level % slabs] = value
                    start_parts(level % slabs)

                @pl.when(owner != place)
                def _():
                    term_ref[level] = value
                    sum_copy(level).start()

        def backward(step, carry):
            level = slices - 1 - step
            real, imag = with_term(level)
            screen_re, screen_im = sincos_small(screen_scale * gathered_ref[level])
            real, imag = real * screen_re + imag * screen_im, imag * screen_re - real * screen_im
            real, imag = filtered(
                real, imag, wave_ref[0], -wave_ref[1], mix_ref
            )
            adjoint_ref[0] = real
            adjoint_ref[1] = imag
            pass_on(level)
            return carry

        lax.fori_loop(0, slices - 1, backward, 0)
        with_term(0)
        pass_on(0)

    @pl.when(worker)
    def _():
        for slab in range(slabs):
            load_slab(slab).wait()
            for step in range(1, members):
                own_copy(slab, step).start()
        work()

    for slab in reversed(range(slabs)):
        value = total_ref[slab, pl.ds(pl.multiple_of(spoke * rows, rows), rows)]
        for step in range(1, angles):
            part_copy(slab, step).wait_recv()
            value = value + part_ref[slab, step]
        out_ref[slab] = value

    for slab in range(slabs):
        for step in range(1, angles):
            part_copy(slab, step).wait_send()

    @pl.when(worker)
    def _():
        for slab in range(slabs):
            for step in range(1, members):
                own_copy(slab, step).wait_send()

        def finish(level, carry):
            owner = level // slabs
            entry = owner % members

            @pl.when((owner >= members) & (entry == place))
            def _():
                if pieces == 2:
                    cross_copy(level).wait_send()
                for step in range(1, members):
                    for number in range(pieces):
                        relay_copy(level, number, step).wait_send()
                sum_copy(level).wait_send()

            @pl.when(entry != place)
            def _():
                term_copy(level).wait_send()

            return carry

        lax.fori_loop(0, slices, finish, 0)


def body(index_change, measured, angle_index, cutoff):
    slabs, width = index_change.shape[0], index_change.shape[1]
    members = measured.shape[0]
    levels, angles = lax.axis_size("depth"), lax.axis_size("angle")
    slices = slabs * levels
    mix, wave = tables(width)
    smem = pl.BlockSpec(memory_space=pltpu.SMEM)
    hbm = pl.BlockSpec(memory_space=pl.ANY)
    sem = pltpu.SemaphoreType.DMA
    return pl.pallas_call(
        kernel,
        out_shape=jax.ShapeDtypeStruct((slabs, width // angles, width), F32),
        in_specs=[smem] * 2 + [hbm] * 4,
        out_specs=pl.BlockSpec(memory_space=pltpu.VMEM),
        scratch_shapes=[
            pltpu.VMEM((width, width), F32),
            pltpu.VMEM((2, width, width), BF16),
            pltpu.VMEM((2, width, width), F32),
            pltpu.VMEM((slices, width, width), F32),
            pltpu.VMEM((slices, 2, width, width), F32),
            pltpu.VMEM((2, width, width), F32),
            pltpu.VMEM((width, width), F32),
            pltpu.VMEM((slices, width, width), F32),
            pltpu.VMEM((slices, members, width, width), F32),
            pltpu.VMEM((slabs, width, width), F32),
            pltpu.VMEM((slabs, angles, width // angles, width), F32),
            sem((slabs, members)),
            sem((slices, 2, members)),
            sem((slices, 2)),
            sem((slices,)),
            sem((slices, members)),
            sem((slices,)),
            sem((slabs,)),
            sem((slabs, angles)),
            sem((slabs, angles)),
            sem((slabs + 3,)),
            pltpu.SemaphoreType.REGULAR,
        ],
        compiler_params=pltpu.CompilerParams(
            collective_id=0, has_side_effects=True, vmem_limit_bytes=60 * 2**20
        ),
    )(angle_index, cutoff, index_change, measured, mix, wave)


def solution(mesh):
    in_specs = (
        P(("blocks", "depth"), None, None),
        P(("blocks", "angle"), None, None),
        P(("blocks", "angle"), None),
        P(),
    )
    out_specs = P(("blocks", "depth"), "angle", None)
    return jax.shard_map(body, mesh=mesh, in_specs=in_specs, out_specs=out_specs, check_vma=False)
```

```python
import math

import jax
import jax.numpy as jnp
import numpy as np
from jax import lax
from jax.experimental import pallas as pl
from jax.experimental.pallas import tpu as pltpu
from jax.sharding import PartitionSpec as P

screen_scale = 0.25
F32 = jnp.float32
BF16 = jnp.bfloat16


def tables(width):
    index = np.arange(width)
    turn = 2.0 * np.pi / width * (index[:, None] * index[None, :] % width)
    hartley = ((np.cos(turn) + np.sin(turn)) / math.sqrt(width)).astype(np.float32)
    high = hartley.astype(BF16)
    low = (hartley - high.astype(np.float32)).astype(BF16)
    freq = (index + width // 2) % width - width // 2
    square = (freq[:, None] ** 2 + freq[None, :] ** 2).astype(np.float64)
    phi = 13.0 / width * (np.sqrt(0.64 * width * width - square) - 0.8 * width)
    wave = np.stack([np.cos(phi), np.sin(phi)]).astype(np.float32)
    return np.stack([high, low]), wave


def halves(value):
    high = value.astype(BF16)
    return high, (value - high.astype(F32)).astype(BF16)


def sincos_small(angle):
    sq = angle * angle
    cosine = 1.0 + sq * (
        -0.5 + sq * (1 / 24 + sq * (-1 / 720 + sq * (1 / 40320 - sq * (1 / 3628800))))
    )
    sine = angle * (
        1.0 + sq * (-1 / 6 + sq * (1 / 120 + sq * (-1 / 5040 + sq * (1 / 362880))))
    )
    return cosine, sine


def sincos_steps(steps, width):
    steps = steps & (width - 1)
    quarter = width // 4
    turns = (steps + quarter // 2) // quarter
    rest = (steps - turns * quarter).astype(F32) * (2.0 * math.pi / width)
    cosine, sine = sincos_small(rest)
    turns = turns & 3
    swap = (turns & 1) == 1
    first = jnp.where(swap, sine, cosine)
    second = jnp.where(swap, cosine, sine)
    first = jnp.where((turns == 1) | (turns == 2), -first, first)
    second = jnp.where(turns >= 2, -second, second)
    return first, second


def columns_mixed(pair, mix_ref):
    high, low = halves(pair)
    return (
        jnp.dot(high, mix_ref[0], preferred_element_type=F32)
        + jnp.dot(low, mix_ref[0], preferred_element_type=F32)
        + jnp.dot(high, mix_ref[1], preferred_element_type=F32)
    )


def rows_mixed(value, mix_ref):
    high, low = halves(value)
    return (
        jnp.dot(mix_ref[0], high, preferred_element_type=F32)
        + jnp.dot(mix_ref[0], low, preferred_element_type=F32)
        + jnp.dot(mix_ref[1], high, preferred_element_type=F32)
    )


def filtered(real, imag, mult_re, mult_im, mix_ref):
    width = real.shape[0]
    mixed = columns_mixed(jnp.concatenate([real, imag], 0), mix_ref)
    real = rows_mixed(mixed[:width], mix_ref)
    imag = rows_mixed(mixed[width:], mix_ref)
    if mult_im is None:
        real, imag = real * mult_re, imag * mult_re
    else:
        real, imag = real * mult_re - imag * mult_im, real * mult_im + imag * mult_re
    real = rows_mixed(real, mix_ref)
    imag = rows_mixed(imag, mix_ref)
    mixed = columns_mixed(jnp.concatenate([real, imag], 0), mix_ref)
    return mixed[:width], mixed[width:]


MESH = pl.DeviceIdType.MESH


def kernel(
    pair_ref, cutoff_ref, index_hbm, target_hbm, mix_hbm, wave_hbm,
    out_ref,
    target_ref, mix_ref, wave_ref, gathered_ref, field_ref, adjoint_ref, square_ref, term_ref, inbox_ref, total_ref, part_ref, mate_ref,
    own_send, relay_send, gather_recv, term_send, term_recv, sum_send, sum_recv,
    part_send, part_recv, pair_send, pair_recv, load_sem, turn_sem,
):
    slabs, width = index_hbm.shape[0], index_hbm.shape[1]
    slices = gathered_ref.shape[0]
    members = target_hbm.shape[0]
    levels, angles = lax.axis_size("depth"), lax.axis_size("angle")
    rows = width // angles
    place, spoke = lax.axis_index("depth"), lax.axis_index("angle")
    worker = place < members
    pieces = 2 - angles % 2
    piece = spoke % pieces
    partner = spoke + 1 - 2 * piece if pieces == 2 else spoke

    def load(number):
        pairs = (
            (mix_hbm, mix_ref),
            (wave_hbm, wave_ref),
            (target_hbm.at[lax.rem(place, members)], target_ref),
        )
        return pltpu.make_async_copy(*pairs[number], load_sem.at[slabs + number])

    def load_slab(slab):
        return pltpu.make_async_copy(
            index_hbm.at[slab], gathered_ref.at[place * slabs + slab], load_sem.at[slab]
        )

    for slab in range(slabs):
        load_slab(slab).start()

    @pl.when(worker)
    def _():
        for number in range(3):
            load(number).start()

    barrier = pltpu.get_barrier_semaphore()
    for step in range(1, levels):
        pl.semaphore_signal(
            barrier, device_id={"depth": lax.rem(place + step, levels)}, device_id_type=MESH
        )
    for step in range(1, angles):
        pl.semaphore_signal(
            barrier, device_id={"angle": lax.rem(spoke + step, angles)}, device_id_type=MESH
        )
    pl.semaphore_wait(barrier, levels + angles - 2)

    def remote(source, target, send, recv, device):
        return pltpu.make_async_remote_copy(
            src_ref=source, dst_ref=target, send_sem=send, recv_sem=recv,
            device_id=device, device_id_type=MESH,
        )

    tall = width // pieces

    def piece_of(level, number):
        return gathered_ref.at[level, pl.ds(pl.multiple_of(number * tall, tall), tall)]

    def own_copy(slab, step):
        level = place * slabs + slab
        return remote(
            gathered_ref.at[level], gathered_ref.at[level], own_send.at[slab, step],
            gather_recv.at[level, 0], {"depth": lax.rem(place + step, members)},
        )

    def own_wait(level):
        remote(
            gathered_ref.at[level], gathered_ref.at[level], relay_send.at[level, 0, 0],
            gather_recv.at[level, 0], {"depth": lax.rem(place + 1, levels)},
        ).wait_recv()

    def entry_copy(slab):
        level = place * slabs + slab
        return remote(
            piece_of(level, piece), piece_of(level, piece), own_send.at[slab, 0],
            gather_recv.at[level, piece], {"depth": lax.rem(place, members)},
        )

    def relay_copy(level, number, step):
        return remote(
            piece_of(level, number), piece_of(level, number),
            relay_send.at[level, number, step], gather_recv.at[level, number],
            {"depth": lax.rem(place + step, members)},
        )

    def cross_copy(level):
        return remote(
            piece_of(level, piece), piece_of(level, piece),
            relay_send.at[level, 0, 0], gather_recv.at[level, piece], {"angle": partner},
        )

    def piece_wait(level, number):
        remote(
            piece_of(level, number), piece_of(level, number), relay_send.at[level, 0, 0],
            gather_recv.at[level, number], {"depth": lax.rem(place + 1, levels)},
        ).wait_recv()

    def term_copy(level):
        entry = (level // slabs) % members
        slot = lax.rem(place - entry + members, members)
        return remote(
            term_ref.at[level], inbox_ref.at[level, slot], term_send.at[level],
            term_recv.at[level, slot], {"depth": entry},
        )

    def sum_copy(level):
        return remote(
            term_ref.at[level], total_ref.at[level % slabs], sum_send.at[level],
            sum_recv.at[level % slabs], {"depth": level // slabs},
        )

    hops = angles // pieces

    def block_of(slab, goal):
        return total_ref.at[slab, pl.ds(pl.multiple_of(goal * rows, rows), rows)]

    def pair_copy(slab, number):
        return remote(
            block_of(slab, 2 * number + 1 - piece), mate_ref.at[slab, number],
            pair_send.at[slab, number], pair_recv.at[slab, number], {"angle": partner},
        )

    def part_copy(slab, step):
        goal = lax.rem(spoke + pieces * step, angles)
        return remote(
            block_of(slab, goal), part_ref.at[slab, step],
            part_send.at[slab, step], part_recv.at[slab, step], {"angle": goal},
        )

    def start_pair(slab):
        if pieces == 2:
            for number in range(hops):
                pair_copy(slab, number).start()

    def start_parts(slab):
        if pieces == 2:
            for number in range(hops):
                pair_copy(slab, number).wait_recv()
                block = block_of(slab, 2 * number + piece)
                block[...] += mate_ref[slab, number]
        for step in range(1, hops):
            part_copy(slab, step).start()

    @pl.when(jnp.logical_not(worker))
    def _():
        for slab in range(slabs):
            load_slab(slab).wait()

        @pl.when(place > members)
        def _():
            pl.semaphore_wait(turn_sem, 1)

        for slab in range(slabs):
            entry_copy(slab).start()
        for slab in range(slabs):
            entry_copy(slab).wait_send()

        @pl.when(place < levels - 1)
        def _():
            pl.semaphore_signal(
                turn_sem, device_id={"depth": lax.rem(place + 1, levels)}, device_id_type=MESH
            )

        for slab in reversed(range(slabs)):
            sum_copy(place * slabs + slab).wait_recv()
            start_pair(slab)
            start_parts(slab)

    def work():
        kx, ky = pair_ref[place, 0], pair_ref[place, 1]
        whole = jnp.full((8, 128), kx * kx + ky * ky, jnp.int32).astype(F32)
        phi = 13.0 / width * (jnp.sqrt(0.64 * width * width - whole) - 0.8 * width)
        lead_re, lead_im = jnp.cos(phi)[:1, :1], jnp.sin(phi)[:1, :1]
        row_re, row_im = sincos_steps(
            kx * lax.broadcasted_iota(jnp.int32, (width, 1), 0), width
        )
        col_re, col_im = sincos_steps(
            ky * lax.broadcasted_iota(jnp.int32, (1, width), 1), width
        )
        row_re, row_im = row_re * lead_re - row_im * lead_im, row_re * lead_im + row_im * lead_re

        def frequency(index):
            return jnp.where(index < width // 2, index, index - width)

        def relay(level):
            owner = level // slabs

            @pl.when((owner >= members) & (owner % members == place) & (level < slices))
            def _():
                piece_wait(level, piece)
                if pieces == 2:
                    cross_copy(level).start()
                for step in range(1, members):
                    relay_copy(level, piece, step).start()

        def second_relay(level):
            owner = level // slabs

            if pieces == 2:
                @pl.when((owner >= members) & (owner % members == place) & (level < slices))
                def _():
                    piece_wait(level, 1 - piece)
                    for step in range(1, members):
                        relay_copy(level, 1 - piece, step).start()

        def ready(level):
            owner = level // slabs

            @pl.when((owner != place) & (owner < members))
            def _():
                own_wait(level)

            @pl.when((owner >= members) & (owner % members != place))
            def _():
                for number in range(pieces):
                    piece_wait(level, number)

        def screened(level, real, imag):
            screen_re, screen_im = sincos_small(screen_scale * gathered_ref[level])
            field_ref[level, 0] = real * screen_re - imag * screen_im
            field_ref[level, 1] = real * screen_im + imag * screen_re

        relay(0)
        relay(1)
        relay(2)
        second_relay(0)
        second_relay(1)
        ready(0)
        screened(0, row_re * col_re - row_im * col_im, row_re * col_im + row_im * col_re)

        def forward(level, carry):
            real, imag = filtered(
                field_ref[level - 1, 0], field_ref[level - 1, 1],
                wave_ref[0], wave_ref[1], mix_ref,
            )
            relay(level + 2)
            second_relay(level + 1)
            ready(level)
            screened(level, real, imag)
            return carry

        for number in range(2):
            load(number).wait()
        lax.fori_loop(1, slices, forward, 0)
        load(2).wait()
        freq_row = frequency(lax.broadcasted_iota(jnp.int32, (width, width), 0))
        freq_col = frequency(lax.broadcasted_iota(jnp.int32, (width, width), 1))
        square_ref[...] = (freq_row * freq_row + freq_col * freq_col).astype(F32)
        cutoff = cutoff_ref[0]
        limit = (cutoff * cutoff).astype(F32)
        adjoint_ref[0] = field_ref[slices - 1, 0]
        adjoint_ref[1] = field_ref[slices - 1, 1]

        def through_pupil(turn, carry):
            pupil = (square_ref[...] <= limit).astype(F32)
            real, imag = filtered(
                adjoint_ref[0], adjoint_ref[1], pupil, None, mix_ref
            )
            misfit = 2.0 * (real * real + imag * imag - target_ref[...])
            misfit = jnp.where(turn == 0, misfit, 1.0)
            adjoint_ref[0] = misfit * real
            adjoint_ref[1] = misfit * imag
            return carry

        lax.fori_loop(0, 2, through_pupil, 0)

        def with_term(level):
            real, imag = adjoint_ref[0], adjoint_ref[1]
            term_ref[level] = screen_scale * (
                field_ref[level, 0] * imag - field_ref[level, 1] * real
            )

            @pl.when((level // slabs) % members != place)
            def _():
                term_copy(level).start()

            return real, imag

        def pass_on(level):
            owner = level // slabs

            @pl.when(owner % members == place)
            def _():
                value = term_ref[level]
                for slot in range(1, members):
                    remote(
                        inbox_ref.at[level, slot], inbox_ref.at[level, slot],
                        term_send.at[level], term_recv.at[level, slot], {"depth": lax.rem(place + 1, levels)},
                    ).wait_recv()
                    value = value + inbox_ref[level, slot]

                @pl.when(owner == place)
                def _():
                    total_ref[level % slabs] = value
                    start_pair(level % slabs)

                @pl.when(owner != place)
                def _():
                    term_ref[level] = value
                    sum_copy(level).start()

        def parts_on(level):
            @pl.when((level // slabs == place) & (level < slices))
            def _():
                start_parts(level % slabs)

        def backward(step, carry):
            level = slices - 1 - step
            real, imag = with_term(level)
            screen_re, screen_im = sincos_small(screen_scale * gathered_ref[level])
            real, imag = real * screen_re + imag * screen_im, imag * screen_re - real * screen_im
            real, imag = filtered(
                real, imag, wave_ref[0], -wave_ref[1], mix_ref
            )
            adjoint_ref[0] = real
            adjoint_ref[1] = imag
            pass_on(level)
            parts_on(level + 1)
            return carry

        lax.fori_loop(0, slices - 1, backward, 0)
        with_term(0)
        pass_on(0)
        parts_on(1)
        parts_on(0)

    @pl.when(worker)
    def _():
        for slab in range(slabs):
            load_slab(slab).wait()
            for step in range(1, members):
                own_copy(slab, step).start()
        work()

    for slab in reversed(range(slabs)):
        value = total_ref[slab, pl.ds(pl.multiple_of(spoke * rows, rows), rows)]
        for step in range(1, hops):
            part_copy(slab, step).wait_recv()
            value = value + part_ref[slab, step]
        out_ref[slab] = value

    for slab in range(slabs):
        for step in range(1, hops):
            part_copy(slab, step).wait_send()
        if pieces == 2:
            for number in range(hops):
                pair_copy(slab, number).wait_send()

    @pl.when(worker)
    def _():
        for slab in range(slabs):
            for step in range(1, members):
                own_copy(slab, step).wait_send()

        def finish(level, carry):
            owner = level // slabs
            entry = owner % members

            @pl.when((owner >= members) & (entry == place))
            def _():
                if pieces == 2:
                    cross_copy(level).wait_send()
                for step in range(1, members):
                    for number in range(pieces):
                        relay_copy(level, number, step).wait_send()
                sum_copy(level).wait_send()

            @pl.when(entry != place)
            def _():
                term_copy(level).wait_send()

            return carry

        lax.fori_loop(0, slices, finish, 0)


def body(index_change, measured, angle_index, cutoff):
    slabs, width = index_change.shape[0], index_change.shape[1]
    members = measured.shape[0]
    levels, angles = lax.axis_size("depth"), lax.axis_size("angle")
    slices = slabs * levels
    mix, wave = tables(width)
    smem = pl.BlockSpec(memory_space=pltpu.SMEM)
    hbm = pl.BlockSpec(memory_space=pl.ANY)
    sem = pltpu.SemaphoreType.DMA
    return pl.pallas_call(
        kernel,
        out_shape=jax.ShapeDtypeStruct((slabs, width // angles, width), F32),
        in_specs=[smem] * 2 + [hbm] * 4,
        out_specs=pl.BlockSpec(memory_space=pltpu.VMEM),
        scratch_shapes=[
            pltpu.VMEM((width, width), F32),
            pltpu.VMEM((2, width, width), BF16),
            pltpu.VMEM((2, width, width), F32),
            pltpu.VMEM((slices, width, width), F32),
            pltpu.VMEM((slices, 2, width, width), F32),
            pltpu.VMEM((2, width, width), F32),
            pltpu.VMEM((width, width), F32),
            pltpu.VMEM((slices, width, width), F32),
            pltpu.VMEM((slices, members, width, width), F32),
            pltpu.VMEM((slabs, width, width), F32),
            pltpu.VMEM((slabs, angles, width // angles, width), F32),
            pltpu.VMEM((slabs, angles, width // angles, width), F32),
            sem((slabs, members)),
            sem((slices, 2, members)),
            sem((slices, 2)),
            sem((slices,)),
            sem((slices, members)),
            sem((slices,)),
            sem((slabs,)),
            sem((slabs, angles)),
            sem((slabs, angles)),
            sem((slabs, angles)),
            sem((slabs, angles)),
            sem((slabs + 3,)),
            pltpu.SemaphoreType.REGULAR,
        ],
        compiler_params=pltpu.CompilerParams(
            collective_id=0, has_side_effects=True, vmem_limit_bytes=60 * 2**20
        ),
    )(angle_index, cutoff, index_change, measured, mix, wave)


def solution(mesh):
    in_specs = (
        P(("blocks", "depth"), None, None),
        P(("blocks", "angle"), None, None),
        P(("blocks", "angle"), None),
        P(),
    )
    out_specs = P(("blocks", "depth"), "angle", None)
    return jax.shard_map(body, mesh=mesh, in_specs=in_specs, out_specs=out_specs, check_vma=False)
```

```python
import math

import jax
import jax.numpy as jnp
import numpy as np
from jax import lax
from jax.experimental import pallas as pl
from jax.experimental.pallas import tpu as pltpu
from jax.sharding import PartitionSpec as P

screen_scale = 0.25
F32 = jnp.float32
BF16 = jnp.bfloat16


def tables(width):
    index = np.arange(width)
    turn = 2.0 * np.pi / width * (index[:, None] * index[None, :] % width)
    hartley = ((np.cos(turn) + np.sin(turn)) / math.sqrt(width)).astype(np.float32)
    high = hartley.astype(BF16)
    low = (hartley - high.astype(np.float32)).astype(BF16)
    freq = (index + width // 2) % width - width // 2
    square = (freq[:, None] ** 2 + freq[None, :] ** 2).astype(np.float64)
    phi = 13.0 / width * (np.sqrt(0.64 * width * width - square) - 0.8 * width)
    wave = np.stack([np.cos(phi), np.sin(phi)]).astype(np.float32)
    return np.stack([high, low]), wave


def halves(value):
    high = value.astype(BF16)
    return high, (value - high.astype(F32)).astype(BF16)


def sincos_small(angle):
    sq = angle * angle
    cosine = 1.0 + sq * (
        -0.5 + sq * (1 / 24 + sq * (-1 / 720 + sq * (1 / 40320 - sq * (1 / 3628800))))
    )
    sine = angle * (
        1.0 + sq * (-1 / 6 + sq * (1 / 120 + sq * (-1 / 5040 + sq * (1 / 362880))))
    )
    return cosine, sine


def sincos_steps(steps, width):
    steps = steps & (width - 1)
    quarter = width // 4
    turns = (steps + quarter // 2) // quarter
    rest = (steps - turns * quarter).astype(F32) * (2.0 * math.pi / width)
    cosine, sine = sincos_small(rest)
    turns = turns & 3
    swap = (turns & 1) == 1
    first = jnp.where(swap, sine, cosine)
    second = jnp.where(swap, cosine, sine)
    first = jnp.where((turns == 1) | (turns == 2), -first, first)
    second = jnp.where(turns >= 2, -second, second)
    return first, second


def columns_mixed(pair, mix_ref):
    high, low = halves(pair)
    return (
        jnp.dot(high, mix_ref[0], preferred_element_type=F32)
        + jnp.dot(low, mix_ref[0], preferred_element_type=F32)
        + jnp.dot(high, mix_ref[1], preferred_element_type=F32)
    )


def rows_mixed(value, mix_ref):
    high, low = halves(value)
    return (
        jnp.dot(mix_ref[0], high, preferred_element_type=F32)
        + jnp.dot(mix_ref[0], low, preferred_element_type=F32)
        + jnp.dot(mix_ref[1], high, preferred_element_type=F32)
    )


def filtered(real, imag, mult_re, mult_im, mix_ref):
    width = real.shape[0]
    mixed = columns_mixed(jnp.concatenate([real, imag], 0), mix_ref)
    real = rows_mixed(mixed[:width], mix_ref)
    imag = rows_mixed(mixed[width:], mix_ref)
    if mult_im is None:
        real, imag = real * mult_re, imag * mult_re
    else:
        real, imag = real * mult_re - imag * mult_im, real * mult_im + imag * mult_re
    real = rows_mixed(real, mix_ref)
    imag = rows_mixed(imag, mix_ref)
    mixed = columns_mixed(jnp.concatenate([real, imag], 0), mix_ref)
    return mixed[:width], mixed[width:]


MESH = pl.DeviceIdType.MESH


def kernel(
    pair_ref, cutoff_ref, index_hbm, target_hbm, mix_hbm, wave_hbm,
    out_ref,
    target_ref, mix_ref, wave_ref, gathered_ref, field_ref, adjoint_ref, square_ref, term_ref, inbox_ref, total_ref, part_ref,
    own_send, relay_send, gather_recv, term_send, term_recv, sum_send, sum_recv,
    part_send, part_recv, load_sem, turn_sem,
):
    slabs, width = index_hbm.shape[0], index_hbm.shape[1]
    slices = gathered_ref.shape[0]
    members = target_hbm.shape[0]
    levels, angles = lax.axis_size("depth"), lax.axis_size("angle")
    rows = width // angles
    place, spoke = lax.axis_index("depth"), lax.axis_index("angle")
    worker = place < members
    pieces = 2 - angles % 2
    piece = spoke % pieces
    partner = spoke + 1 - 2 * piece if pieces == 2 else spoke

    def load(number):
        pairs = (
            (mix_hbm, mix_ref),
            (wave_hbm, wave_ref),
            (target_hbm.at[lax.rem(place, members)], target_ref),
        )
        return pltpu.make_async_copy(*pairs[number], load_sem.at[slabs + number])

    def load_slab(slab):
        return pltpu.make_async_copy(
            index_hbm.at[slab], gathered_ref.at[place * slabs + slab], load_sem.at[slab]
        )

    for slab in range(slabs):
        load_slab(slab).start()

    @pl.when(worker)
    def _():
        for number in range(3):
            load(number).start()

    barrier = pltpu.get_barrier_semaphore()
    for step in range(1, levels):
        pl.semaphore_signal(
            barrier, device_id={"depth": lax.rem(place + step, levels)}, device_id_type=MESH
        )
    for step in range(1, angles):
        pl.semaphore_signal(
            barrier, device_id={"angle": lax.rem(spoke + step, angles)}, device_id_type=MESH
        )
    pl.semaphore_wait(barrier, levels + angles - 2)

    def remote(source, target, send, recv, device):
        return pltpu.make_async_remote_copy(
            src_ref=source, dst_ref=target, send_sem=send, recv_sem=recv,
            device_id=device, device_id_type=MESH,
        )

    tall = width // pieces

    def piece_of(level, number):
        return gathered_ref.at[level, pl.ds(pl.multiple_of(number * tall, tall), tall)]

    def own_copy(slab, step):
        level = place * slabs + slab
        return remote(
            gathered_ref.at[level], gathered_ref.at[level], own_send.at[slab, step],
            gather_recv.at[level, 0], {"depth": lax.rem(place + step, members)},
        )

    def own_wait(level):
        remote(
            gathered_ref.at[level], gathered_ref.at[level], relay_send.at[level, 0, 0],
            gather_recv.at[level, 0], {"depth": lax.rem(place + 1, levels)},
        ).wait_recv()

    def entry_copy(slab):
        level = place * slabs + slab
        return remote(
            piece_of(level, piece), piece_of(level, piece), own_send.at[slab, 0],
            gather_recv.at[level, piece], {"depth": lax.rem(place, members)},
        )

    def relay_copy(level, number, step):
        return remote(
            piece_of(level, number), piece_of(level, number),
            relay_send.at[level, number, step], gather_recv.at[level, number],
            {"depth": lax.rem(place + step, members)},
        )

    def cross_copy(level):
        return remote(
            piece_of(level, piece), piece_of(level, piece),
            relay_send.at[level, 0, 0], gather_recv.at[level, piece], {"angle": partner},
        )

    def piece_wait(level, number):
        remote(
            piece_of(level, number), piece_of(level, number), relay_send.at[level, 0, 0],
            gather_recv.at[level, number], {"depth": lax.rem(place + 1, levels)},
        ).wait_recv()

    def term_copy(level):
        entry = (level // slabs) % members
        slot = lax.rem(place - entry + members, members)
        return remote(
            term_ref.at[level], inbox_ref.at[level, slot], term_send.at[level],
            term_recv.at[level, slot], {"depth": entry},
        )

    def sum_copy(level):
        return remote(
            term_ref.at[level], total_ref.at[level % slabs], sum_send.at[level],
            sum_recv.at[level % slabs], {"depth": level // slabs},
        )

    def part_copy(slab, step):
        goal = lax.rem(spoke + step, angles)
        return remote(
            total_ref.at[slab, pl.ds(pl.multiple_of(goal * rows, rows), rows)],
            part_ref.at[slab, step], part_send.at[slab, step], part_recv.at[slab, step],
            {"angle": goal},
        )

    def start_parts(slab):
        for step in range(1, angles):
            part_copy(slab, step).start()

    @pl.when(jnp.logical_not(worker))
    def _():
        for slab in range(slabs):
            load_slab(slab).wait()

        @pl.when(place > members)
        def _():
            pl.semaphore_wait(turn_sem, 1)

        for slab in range(slabs):
            entry_copy(slab).start()
        for slab in range(slabs):
            entry_copy(slab).wait_send()

        @pl.when(place < levels - 1)
        def _():
            pl.semaphore_signal(
                turn_sem, device_id={"depth": lax.rem(place + 1, levels)}, device_id_type=MESH
            )

        for slab in reversed(range(slabs)):
            sum_copy(place * slabs + slab).wait_recv()
            start_parts(slab)

    def work():
        kx, ky = pair_ref[place, 0], pair_ref[place, 1]
        whole = jnp.full((8, 128), kx * kx + ky * ky, jnp.int32).astype(F32)
        phi = 13.0 / width * (jnp.sqrt(0.64 * width * width - whole) - 0.8 * width)
        lead_re, lead_im = jnp.cos(phi)[:1, :1], jnp.sin(phi)[:1, :1]
        row_re, row_im = sincos_steps(
            kx * lax.broadcasted_iota(jnp.int32, (width, 1), 0), width
        )
        col_re, col_im = sincos_steps(
            ky * lax.broadcasted_iota(jnp.int32, (1, width), 1), width
        )
        row_re, row_im = row_re * lead_re - row_im * lead_im, row_re * lead_im + row_im * lead_re

        def frequency(index):
            return jnp.where(index < width // 2, index, index - width)

        def relay(level):
            owner = level // slabs

            @pl.when((owner >= members) & (owner % members == place) & (level < slices))
            def _():
                piece_wait(level, piece)
                if pieces == 2:
                    cross_copy(level).start()
                for step in range(1, members):
                    relay_copy(level, piece, step).start()

        def second_relay(level):
            owner = level // slabs

            if pieces == 2:
                @pl.when((owner >= members) & (owner % members == place) & (level < slices))
                def _():
                    piece_wait(level, 1 - piece)
                    for step in range(1, members):
                        relay_copy(level, 1 - piece, step).start()

        def ready(level):
            owner = level // slabs

            @pl.when((owner != place) & (owner < members))
            def _():
                own_wait(level)

            @pl.when((owner >= members) & (owner % members != place))
            def _():
                for number in range(pieces):
                    piece_wait(level, number)

        def screened(level, real, imag):
            screen_re, screen_im = sincos_small(screen_scale * gathered_ref[level])
            inbox_ref[level, 0] = screen_re
            term_ref[level] = screen_im
            field_ref[level, 0] = real * screen_re - imag * screen_im
            field_ref[level, 1] = real * screen_im + imag * screen_re

        relay(0)
        relay(1)
        relay(2)
        second_relay(0)
        second_relay(1)
        ready(0)
        screened(0, row_re * col_re - row_im * col_im, row_re * col_im + row_im * col_re)

        def forward(level, carry):
            real, imag = filtered(
                field_ref[level - 1, 0], field_ref[level - 1, 1],
                wave_ref[0], wave_ref[1], mix_ref,
            )
            relay(level + 2)
            second_relay(level + 1)
            ready(level)
            screened(level, real, imag)
            return carry

        for number in range(2):
            load(number).wait()
        lax.fori_loop(1, slices, forward, 0)
        load(2).wait()
        freq_row = frequency(lax.broadcasted_iota(jnp.int32, (width, width), 0))
        freq_col = frequency(lax.broadcasted_iota(jnp.int32, (width, width), 1))
        square_ref[...] = (freq_row * freq_row + freq_col * freq_col).astype(F32)
        cutoff = cutoff_ref[0]
        limit = (cutoff * cutoff).astype(F32)
        adjoint_ref[0] = field_ref[slices - 1, 0]
        adjoint_ref[1] = field_ref[slices - 1, 1]

        def through_pupil(turn, carry):
            pupil = (square_ref[...] <= limit).astype(F32)
            real, imag = filtered(
                adjoint_ref[0], adjoint_ref[1], pupil, None, mix_ref
            )
            misfit = 2.0 * (real * real + imag * imag - target_ref[...])
            misfit = jnp.where(turn == 0, misfit, 1.0)
            adjoint_ref[0] = misfit * real
            adjoint_ref[1] = misfit * imag
            return carry

        lax.fori_loop(0, 2, through_pupil, 0)

        def with_term(level):
            real, imag = adjoint_ref[0], adjoint_ref[1]
            term_ref[level] = screen_scale * (
                field_ref[level, 0] * imag - field_ref[level, 1] * real
            )

            @pl.when((level // slabs) % members != place)
            def _():
                term_copy(level).start()

            return real, imag

        def pass_on(level):
            owner = level // slabs

            @pl.when(owner % members == place)
            def _():
                value = term_ref[level]
                for slot in range(1, members):
                    remote(
                        inbox_ref.at[level, slot], inbox_ref.at[level, slot],
                        term_send.at[level], term_recv.at[level, slot], {"depth": lax.rem(place + 1, levels)},
                    ).wait_recv()
                    value = value + inbox_ref[level, slot]

                @pl.when(owner == place)
                def _():
                    total_ref[level % slabs] = value
                    start_parts(level % slabs)

                @pl.when(owner != place)
                def _():
                    term_ref[level] = value
                    sum_copy(level).start()

        def backward(step, carry):
            level = slices - 1 - step
            screen_re, screen_im = inbox_ref[level, 0], term_ref[level]
            real, imag = with_term(level)
            real, imag = real * screen_re + imag * screen_im, imag * screen_re - real * screen_im
            real, imag = filtered(
                real, imag, wave_ref[0], -wave_ref[1], mix_ref
            )
            adjoint_ref[0] = real
            adjoint_ref[1] = imag
            pass_on(level)
            return carry

        lax.fori_loop(0, slices - 1, backward, 0)
        with_term(0)
        pass_on(0)

    @pl.when(worker)
    def _():
        for slab in range(slabs):
            load_slab(slab).wait()
            for step in range(1, members):
                own_copy(slab, step).start()
        work()

    for slab in reversed(range(slabs)):
        value = total_ref[slab, pl.ds(pl.multiple_of(spoke * rows, rows), rows)]
        for step in range(1, angles):
            part_copy(slab, step).wait_recv()
            value = value + part_ref[slab, step]
        out_ref[slab] = value

    for slab in range(slabs):
        for step in range(1, angles):
            part_copy(slab, step).wait_send()

    @pl.when(worker)
    def _():
        for slab in range(slabs):
            for step in range(1, members):
                own_copy(slab, step).wait_send()

        def finish(level, carry):
            owner = level // slabs
            entry = owner % members

            @pl.when((owner >= members) & (entry == place))
            def _():
                if pieces == 2:
                    cross_copy(level).wait_send()
                for step in range(1, members):
                    for number in range(pieces):
                        relay_copy(level, number, step).wait_send()
                sum_copy(level).wait_send()

            @pl.when(entry != place)
            def _():
                term_copy(level).wait_send()

            return carry

        lax.fori_loop(0, slices, finish, 0)


def body(index_change, measured, angle_index, cutoff):
    slabs, width = index_change.shape[0], index_change.shape[1]
    members = measured.shape[0]
    levels, angles = lax.axis_size("depth"), lax.axis_size("angle")
    slices = slabs * levels
    mix, wave = tables(width)
    smem = pl.BlockSpec(memory_space=pltpu.SMEM)
    hbm = pl.BlockSpec(memory_space=pl.ANY)
    sem = pltpu.SemaphoreType.DMA
    return pl.pallas_call(
        kernel,
        out_shape=jax.ShapeDtypeStruct((slabs, width // angles, width), F32),
        in_specs=[smem] * 2 + [hbm] * 4,
        out_specs=pl.BlockSpec(memory_space=pltpu.VMEM),
        scratch_shapes=[
            pltpu.VMEM((width, width), F32),
            pltpu.VMEM((2, width, width), BF16),
            pltpu.VMEM((2, width, width), F32),
            pltpu.VMEM((slices, width, width), F32),
            pltpu.VMEM((slices, 2, width, width), F32),
            pltpu.VMEM((2, width, width), F32),
            pltpu.VMEM((width, width), F32),
            pltpu.VMEM((slices, width, width), F32),
            pltpu.VMEM((slices, members, width, width), F32),
            pltpu.VMEM((slabs, width, width), F32),
            pltpu.VMEM((slabs, angles, width // angles, width), F32),
            sem((slabs, members)),
            sem((slices, 2, members)),
            sem((slices, 2)),
            sem((slices,)),
            sem((slices, members)),
            sem((slices,)),
            sem((slabs,)),
            sem((slabs, angles)),
            sem((slabs, angles)),
            sem((slabs + 3,)),
            pltpu.SemaphoreType.REGULAR,
        ],
        compiler_params=pltpu.CompilerParams(
            collective_id=0, has_side_effects=True, vmem_limit_bytes=60 * 2**20
        ),
    )(angle_index, cutoff, index_change, measured, mix, wave)


def solution(mesh):
    in_specs = (
        P(("blocks", "depth"), None, None),
        P(("blocks", "angle"), None, None),
        P(("blocks", "angle"), None),
        P(),
    )
    out_specs = P(("blocks", "depth"), "angle", None)
    return jax.shard_map(body, mesh=mesh, in_specs=in_specs, out_specs=out_specs, check_vma=False)
```
